32 devices in a mesh: dp: 4 (over z), ctx: 8 (over y, x, core).
Axes of the slice: x: 2, y: 2, z: 4, core: 2. Of those that a mesh axis runs over, the one named last changes fastest.
Arguments:
- query_heads: bfloat16 [4, 1024, 1024], P('dp', 'ctx'), may hold values from -6 to 6
- key_heads: bfloat16 [4, 1024, 1024], P('dp', 'ctx'), may hold values from -6 to 6
- value_heads: bfloat16 [4, 1024, 1024], P('dp', 'ctx'), may hold values from -6 to 6
- grad_output: bfloat16 [4, 1024, 1024], P('dp', 'ctx'), may hold values from -6 to 6
- layer_input: bfloat16 [4, 1024, 1152], P('dp', 'ctx'), may hold values from -6 to 6
Outputs:
- grad_query: bfloat16 [4, 1024, 1024], P('dp', 'ctx')
- grad_key: bfloat16 [4, 1024, 1024], P('dp', 'ctx')
- grad_value: bfloat16 [4, 1024, 1024], P('dp', 'ctx')
- grad_weight: float32 [1152, 1024], P('dp', 'ctx')
The draws below stay inside these ranges and needn't reach their ends.
All inputs are finite; a program needn't handle non-finite values.
Results may differ from the reference program's by a relative error of at most 0.008.
Values sent between devices are 32-bit elements; how exact they have to be, the bound alone decides.
A program may use at most 128 MiB of HBM per device.

```python
import math
import jax
import jax.numpy as jnp
from jax import lax

HD = 128
HV = 8
DW = 1152
TOK_DEV = 128
VW = 1024
SEQ = 1024
BATCH = 4
N_DP = 4


def block_levels(rng, dims, cuts, smallest, high):
    loudness, own = 1.0, jax.random.fold_in(rng, 6)
    for axis_at, shards_of in cuts:
        heights = jnp.exp(jax.random.uniform(jax.random.fold_in(own, axis_at), (shards_of,), jnp.float32, smallest / len(cuts), high / len(cuts)))
        loudness = loudness * jnp.repeat(heights, dims[axis_at] // shards_of).reshape([-1 if axis == axis_at else 1 for axis in range(len(dims))])
    return loudness


def normal_values(rng, extent, scale, most, pieces=(), held_as=jnp.bfloat16):
    level = block_levels(rng, extent, pieces, -0.22, 0.18) if pieces else 1.0
    values = jax.random.normal(rng, extent, jnp.float32) * scale * level
    return jnp.minimum(jnp.maximum(values, -most), most).astype(held_as)


def setup_inputs(seed: int = 0) -> dict:
    streams_of = jax.random.split(jax.random.key(seed), 6)
    query_heads = normal_values(streams_of[0], (BATCH, SEQ, VW), 1.0, 6.0, ((0, 4), (1, 8)))
    key_heads = normal_values(streams_of[1], (BATCH, SEQ, VW), 1.0, 6.0, ((0, 4), (1, 8)))
    value_heads = normal_values(streams_of[2], (BATCH, SEQ, VW), 1.0, 6.0, ((0, 4), (1, 8)))
    grad_output = normal_values(streams_of[3], (BATCH, SEQ, VW), 1.0, 6.0, ((0, 4), (1, 8)))
    layer_input = normal_values(streams_of[4], (BATCH, SEQ, DW), 1.0, 6.0, ((0, 4), (1, 8)))
    return {"query_heads": query_heads, "key_heads": key_heads, "value_heads": value_heads, "grad_output": grad_output, "layer_input": layer_input}


def reference(query_heads, key_heads, value_heads, grad_output, layer_input):
    length = query_heads.shape[1]
    blocks = length // TOK_DEV
    scale = 1.0 / math.sqrt(HD * length)
    rscale = 1.0 / math.sqrt(N_DP * length)
    highest = lax.Precision.HIGHEST
    rows = jnp.arange(TOK_DEV)
    causal = (rows[:, None] >= rows[None, :]).astype(jnp.float32)

    def split(array):
        return array.reshape(blocks, TOK_DEV, HV, HD).astype(jnp.float32)

    def one(total, items):
        query, keyed, valued, cotan, inputs = items
        qf, kf, vf, gf = (split(query), split(keyed), split(valued), split(cotan))
        kv_block = jnp.einsum('bthi,bthj->bhij', kf, vf, precision=highest)
        qg_block = jnp.einsum('bthi,bthj->bhij', qf, gf, precision=highest)
        zero = jnp.zeros((1, HV, HD, HD), jnp.float32)
        prefix = jnp.concatenate([zero, jnp.cumsum(kv_block, 0)[:-1]], 0)
        suffix = jnp.concatenate([jnp.cumsum(qg_block[::-1], 0)[:-1][::-1], zero], 0)
        score_raw = jnp.einsum('bthd,bshd->bhts', qf, kf, precision=highest)
        grad_raw = jnp.einsum('bthd,bshd->bhts', gf, vf, precision=highest)
        score_w = (scale * score_raw * causal).astype(jnp.bfloat16).astype(jnp.float32)
        grad_w = (scale * grad_raw * causal).astype(jnp.bfloat16).astype(jnp.float32)
        dquery = jnp.einsum('bhts,bshd->bthd', grad_w, kf, precision=highest)
        dquery = dquery + scale * jnp.einsum('bthj,bhij->bthi', gf, prefix, precision=highest)
        dkey = jnp.einsum('bhts,bthd->bshd', grad_w, qf, precision=highest)
        dkey = dkey + scale * jnp.einsum('bshj,bhij->bshi', vf, suffix, precision=highest)
        dvalue = jnp.einsum('bhts,bthd->bshd', score_w, gf, precision=highest)
        dvalue = dvalue + scale * jnp.einsum('bshi,bhij->bshj', kf, suffix, precision=highest)
        dquery = dquery.reshape(length, HV * HD).astype(jnp.bfloat16)
        dkey = dkey.reshape(length, HV * HD).astype(jnp.bfloat16)
        dvalue = dvalue.reshape(length, HV * HD).astype(jnp.bfloat16)
        total = total + jnp.dot(inputs.T, dvalue, preferred_element_type=jnp.float32)
        return (total, (dquery, dkey, dvalue))
    start = jnp.zeros((layer_input.shape[2], query_heads.shape[2]), jnp.float32)
    total, grads = lax.scan(one, start, (query_heads, key_heads, value_heads, grad_output, layer_input))
    return (grads[0], grads[1], grads[2], total * rscale)
```

```python
import functools
import math

import jax
import jax.numpy as jnp
from jax import lax
from jax.experimental import pallas as pl
from jax.experimental.pallas import tpu as pltpu
from jax.sharding import PartitionSpec as P

HD = 128
NN = (((1,), (0,)), ((), ()))
NT = (((1,), (1,)), ((), ()))
TN = (((0,), (0,)), ((), ()))


def dot(a, b, dims):
    return lax.dot_general(a, b, dims, preferred_element_type=jnp.float32)


def kernel(
    n, m, scale, rscale,
    q, k, v, g, x,
    dq, dk, dv, w,
    xg, xb, st, sib, tot, srecv, ext, acc, dvs, dvg, wt, wrecv,
    x_send, x_recv, p_send, p_recv, s_send, s_recv, e_send, e_recv,
    d_send, d_recv, w_send, w_recv,
):
    length, width = q.shape
    heads = width // HD
    half = heads // 2
    chips = n // 2
    cb = dvs.shape[2]
    rows = wt.shape[1]
    part = length // 2
    bits = n.bit_length() - 1
    me = lax.axis_index("ctx")
    row = lax.axis_index("dp")
    core = lax.rem(me, 2)
    chip = me // 2
    sibling = me + 1 - 2 * core

    def flip(index, mask):
        out = index
        for b in range(bits):
            if mask >> b & 1:
                out = out + (1 << b) * (1 - 2 * lax.rem(me // (1 << b), 2))
        return out

    def remote(src, dst, send, recv, to):
        return pltpu.make_async_remote_copy(
            src_ref=src, dst_ref=dst, send_sem=send, recv_sem=recv,
            device_id=to, device_id_type=pl.DeviceIdType.MESH,
        )

    orders = ([*range(1, bits), 0], [*range(bits - 1, 0, -1), 0])

    def x_copy(s, mask, b):
        slot = flip(me, mask)
        ref = xg.at[slot, pl.ds(s * part, part)]
        got = mask | (1 << b)
        return remote(
            ref, ref, x_send.at[s, got], x_recv.at[s, got], {"ctx": flip(me, 1 << b)}
        )

    def reached(s, mask):
        return max([i + 1 for i, b in enumerate(orders[s]) if mask >> b & 1], default=0)

    def x_wait(s, mask):
        last = orders[s][reached(s, mask) - 1]
        x_copy(s, mask ^ (1 << last), last).wait_recv()

    def x_forward(s, mask):
        for b in orders[s][reached(s, mask):]:
            x_copy(s, mask, b).start()

    barrier = pltpu.get_barrier_semaphore()
    for j in range(1, n):
        pl.semaphore_signal(
            barrier, inc=1, device_id={"ctx": lax.rem(me + j, n)},
            device_id_type=pl.DeviceIdType.MESH,
        )
    for j in range(1, m):
        pl.semaphore_signal(
            barrier, inc=1, device_id={"dp": lax.rem(row + j, m)},
            device_id_type=pl.DeviceIdType.MESH,
        )

    def cols(h):
        return slice(h * HD, (h + 1) * HD)

    for h in range(heads):
        a, i = h // half, h % half
        st[a, 0, i] = dot(k[:, cols(h)], v[:, cols(h)], TN)
        st[a, 1, i] = dot(q[:, cols(h)], g[:, cols(h)], TN)
    xg[me] = x[...].astype(jnp.float32)
    pl.semaphore_wait(barrier, n - 1 + m - 1)

    pair = [
        remote(st.at[1 - core], sib.at[1 - core], p_send.at[0], p_recv.at[0], {"ctx": sibling}),
        remote(st.at[core], sib.at[core], p_send.at[1], p_recv.at[1], {"ctx": sibling}),
    ]
    pair_in = remote(st.at[core], sib.at[core], p_send.at[0], p_recv.at[0], {"ctx": sibling})
    for c in pair:
        c.start()
    for s in range(2):
        x_copy(s, 0, orders[s][0]).start()
    pair_in.wait_recv()
    tot[...] = st[core] + sib[core]
    states = []
    for j in range(1, chips):
        wrap = (chip + j) // chips
        to = (chip + j - chips * wrap) * 2 + core
        c = remote(tot.at[wrap], srecv.at[j - 1], s_send.at[j - 1], s_recv.at[j - 1], {"ctx": to})
        c.start()
        states.append(c)
    for s in range(2):
        for b in orders[s][1:]:
            x_copy(s, 0, b).start()

    at_row = lax.broadcasted_iota(jnp.int32, (length, length), 0)
    at_col = lax.broadcasted_iota(jnp.int32, (length, length), 1)
    lower = at_row >= at_col
    upper = at_row <= at_col
    for h in range(heads):
        qh, kh, vh, gh = (r[:, cols(h)] for r in (q, k, v, g))
        score_t = jnp.where(upper, scale * dot(kh, qh, NT), 0.0).astype(jnp.bfloat16)
        grad = jnp.where(lower, scale * dot(gh, vh, NT), 0.0).astype(jnp.bfloat16)
        acc[0, :, cols(h)] = dot(grad, kh, NN)
        acc[1, :, cols(h)] = dot(grad, qh, TN)
        acc[2, :, cols(h)] = dot(score_t, gh, NN)

    if bits > 1:
        for s in range(2):
            mask = 1 << orders[s][0]
            x_wait(s, mask)
            x_forward(s, mask)

    ext[core] = jnp.zeros_like(tot)
    for j in range(1, chips):
        kind = 1 - (chip - j + chips) // chips
        states[j - 1].wait_recv()
        ext[core, kind] += srecv[j - 1]
    share = remote(ext.at[core], ext.at[core], e_send, e_recv, {"ctx": sibling})
    share_in = remote(ext.at[1 - core], ext.at[1 - core], e_send, e_recv, {"ctx": sibling})
    share.start()
    pair_rest = remote(st.at[1 - core], sib.at[1 - core], p_send.at[1], p_recv.at[1], {"ctx": sibling})
    pair_rest.wait_recv()
    share_in.wait_recv()

    second = core.astype(jnp.float32)
    first = 1.0 - second

    def suffix(h):
        a, i = h // half, h % half
        return (scale * (ext[a, 1, i] + first * sib[a, 1, i])).astype(jnp.bfloat16)

    def prefix(h):
        a, i = h // half, h % half
        return (scale * (ext[a, 0, i] + second * sib[a, 0, i])).astype(jnp.bfloat16)

    for h in range(heads):
        out = acc[2, :, cols(h)] + dot(k[:, cols(h)], suffix(h), NN)
        dv[:, cols(h)] = out.astype(jnp.bfloat16)
    for j in range(n):
        dvs[j] = dv[:, j * cb:(j + 1) * cb].astype(jnp.float32)
    values = []
    for j in range(1, n):
        to = lax.rem(me + j, n)
        c = remote(dvs.at[to], dvg.at[me], d_send.at[j - 1], d_recv.at[j - 1], {"ctx": to})
        c.start()
        values.append(c)
    dvg[me] = dvs[me]

    waited = [{1 << orders[s][0]} if bits > 1 else set() for s in range(2)]
    for i in range(1, bits - 1):
        for s in range(2):
            for mask in range(n):
                if reached(s, mask) == i + 1:
                    x_wait(s, mask)
                    x_forward(s, mask)
                    waited[s].add(mask)

    for h in range(heads):
        out = acc[0, :, cols(h)] + dot(g[:, cols(h)], prefix(h), NT)
        dq[:, cols(h)] = out.astype(jnp.bfloat16)
        out = acc[1, :, cols(h)] + dot(v[:, cols(h)], suffix(h), NT)
        dk[:, cols(h)] = out.astype(jnp.bfloat16)

    for mask in range(n):
        for s in range(2):
            if mask and mask not in waited[s]:
                x_wait(s, mask)
        slot = flip(me, mask)
        xb[slot] = xg[slot].astype(jnp.bfloat16)
    for j in range(1, n):
        came = lax.rem(me - j + n, n)
        remote(dvs.at[came], dvg.at[came], d_send.at[j - 1], d_recv.at[j - 1], {"ctx": came}).wait_recv()

    across = dvg[...].reshape(n * length, cb).astype(jnp.bfloat16)
    down = xb[...].reshape(n * length, xb.shape[2])
    total = jnp.transpose(dot(across, down, TN))
    for d in range(m):
        wt[d] = total[d * rows:(d + 1) * rows]
    weights = []
    for j in range(1, m):
        to = lax.rem(row + j, m)
        c = remote(wt.at[to], wrecv.at[j - 1], w_send.at[j - 1], w_recv.at[j - 1], {"dp": to})
        c.start()
        weights.append(c)
    out = wt[row]
    for c in weights:
        c.wait_recv()
    for j in range(1, m):
        out = out + wrecv[j - 1]
    w[...] = out * rscale

    for c in pair + states + [share] + values + weights:
        c.wait_send()
    for s in range(2):
        for mask in range(n):
            for b in orders[s][reached(s, mask):]:
                x_copy(s, mask, b).wait_send()


def on_device(query_heads, key_heads, value_heads, grad_output, layer_input):
    length, width = query_heads.shape[1:]
    wide = layer_input.shape[2]
    n = lax.axis_size("ctx")
    m = lax.axis_size("dp")
    scale = 1.0 / math.sqrt(HD * length * n)
    rscale = 1.0 / math.sqrt(m * length * n)
    heads, chips, cb, rows = width // HD, n // 2, width // n, wide // m
    half = heads // 2
    f32, bf16 = jnp.float32, jnp.bfloat16
    vmem = pl.BlockSpec(memory_space=pltpu.VMEM)
    dma = pltpu.SemaphoreType.DMA
    out = jax.ShapeDtypeStruct((length, width), bf16)
    dq, dk, dv, w = pl.pallas_call(
        functools.partial(kernel, n, m, scale, rscale),
        out_shape=(out, out, out, jax.ShapeDtypeStruct((rows, cb), f32)),
        in_specs=[vmem] * 5,
        out_specs=(vmem,) * 4,
        scratch_shapes=[
            pltpu.VMEM((n, length, wide), f32),
            pltpu.VMEM((n, length, wide), bf16),
            pltpu.VMEM((2, 2, half, HD, HD), f32),
            pltpu.VMEM((2, 2, half, HD, HD), f32),
            pltpu.VMEM((2, half, HD, HD), f32),
            pltpu.VMEM((max(chips - 1, 1), half, HD, HD), f32),
            pltpu.VMEM((2, 2, half, HD, HD), f32),
            pltpu.VMEM((3, length, width), f32),
            pltpu.VMEM((n, length, cb), f32),
            pltpu.VMEM((n, length, cb), f32),
            pltpu.VMEM((m, rows, cb), f32),
            pltpu.VMEM((max(m - 1, 1), rows, cb), f32),
            dma((2, n)), dma((2, n)),
            dma((2,)), dma((2,)),
            dma((max(chips - 1, 1),)), dma((max(chips - 1, 1),)),
            dma, dma,
            dma((n - 1,)), dma((n - 1,)),
            dma((max(m - 1, 1),)), dma((max(m - 1, 1),)),
        ],
        compiler_params=pltpu.CompilerParams(
            collective_id=0, has_side_effects=True, vmem_limit_bytes=56 * 2**20
        ),
    )(query_heads[0], key_heads[0], value_heads[0], grad_output[0], layer_input[0])
    return dq[None], dk[None], dv[None], w


def solution(mesh):
    spec = P("dp", "ctx", None)
    return jax.shard_map(
        on_device, mesh=mesh, in_specs=(spec,) * 5,
        out_specs=(spec, spec, spec, P("dp", "ctx")), check_vma=False,
    )
```

```python
import functools
import math

import jax
import jax.numpy as jnp
from jax import lax
from jax.experimental import pallas as pl
from jax.experimental.pallas import tpu as pltpu
from jax.sharding import PartitionSpec as P

HD = 128
NN = (((1,), (0,)), ((), ()))
NT = (((1,), (1,)), ((), ()))
TN = (((0,), (0,)), ((), ()))


def dot(a, b, dims):
    return lax.dot_general(a, b, dims, preferred_element_type=jnp.float32)


def kernel(
    n, m, scale, rscale,
    q, k, v, g, x,
    dq, dk, dv, w,
    xs, xsib, xt, st, sib, tot, srecv, ext, acc, dvs, dvr, wt, wr, wrecv,
    x_send, x_recv, p_send, p_recv, s_send, s_recv, e_send, e_recv,
    d_send, d_recv, r_send, r_recv, w_send, w_recv,
):
    length, width = q.shape
    heads = width // HD
    half = heads // 2
    chips = n // 2
    cb = dvs.shape[3]
    rows = w.shape[0]
    part = rows // 2
    bits = chips.bit_length() - 1
    me = lax.axis_index("ctx")
    row = lax.axis_index("dp")
    core = lax.rem(me, 2)
    chip = me // 2
    sibling = me + 1 - 2 * core

    def flip(mask):
        out = chip
        for b in range(bits):
            if mask >> b & 1:
                out = out + (1 << b) * (1 - 2 * lax.rem(chip // (1 << b), 2))
        return out

    def remote(src, dst, send, recv, to):
        return pltpu.make_async_remote_copy(
            src_ref=src, dst_ref=dst, send_sem=send, recv_sem=recv,
            device_id=to, device_id_type=pl.DeviceIdType.MESH,
        )

    orders = ([*range(bits)], [*range(bits - 1, -1, -1)])

    def place(s, mask):
        return sum((mask >> b & 1) << (bits - 1 - i) for i, b in enumerate(orders[s]))

    barrier = pltpu.get_barrier_semaphore()
    for j in range(1, n):
        pl.semaphore_signal(
            barrier, inc=1, device_id={"ctx": lax.rem(me + j, n)},
            device_id_type=pl.DeviceIdType.MESH,
        )
    for j in range(1, m):
        pl.semaphore_signal(
            barrier, inc=1, device_id={"dp": lax.rem(row + j, m)},
            device_id_type=pl.DeviceIdType.MESH,
        )

    def cols(h):
        return slice(h * HD, (h + 1) * HD)

    for h in range(heads):
        a, i = h // half, h % half
        st[a, 0, i] = dot(k[:, cols(h)], v[:, cols(h)], TN)
        st[a, 1, i] = dot(q[:, cols(h)], g[:, cols(h)], TN)
    xs[...] = x[...].astype(jnp.float32)
    pl.semaphore_wait(barrier, n - 1 + m - 1)

    pair = [
        remote(st.at[1 - core], sib.at[1 - core], p_send.at[0], p_recv.at[0], {"ctx": sibling}),
        remote(st.at[core], sib.at[core], p_send.at[1], p_recv.at[1], {"ctx": sibling}),
    ]
    pair_in = remote(st.at[core], sib.at[core], p_send.at[0], p_recv.at[0], {"ctx": sibling})
    for c in pair:
        c.start()
    x_pair = remote(xs, xsib, x_send, x_recv, {"ctx": sibling})
    pair_in.wait_recv()
    tot[...] = st[core] + sib[core]
    states = []
    for j in range(1, chips):
        wrap = (chip + j) // chips
        to = (chip + j - chips * wrap) * 2 + core
        c = remote(tot.at[wrap], srecv.at[j - 1], s_send.at[j - 1], s_recv.at[j - 1], {"ctx": to})
        c.start()
        states.append(c)
    x_pair.start()

    at_row = lax.broadcasted_iota(jnp.int32, (length, length), 0)
    at_col = lax.broadcasted_iota(jnp.int32, (length, length), 1)
    lower = at_row >= at_col
    upper = at_row <= at_col
    for h in range(heads):
        qh, kh, vh, gh = (r[:, cols(h)] for r in (q, k, v, g))
        score_t = jnp.where(upper, scale * dot(kh, qh, NT), 0.0).astype(jnp.bfloat16)
        grad = jnp.where(lower, scale * dot(gh, vh, NT), 0.0).astype(jnp.bfloat16)
        acc[0, :, cols(h)] = dot(grad, kh, NN)
        acc[1, :, cols(h)] = dot(grad, qh, TN)
        acc[2, :, cols(h)] = dot(score_t, gh, NN)

    xt[:, :length] = jnp.transpose(xs[...]).astype(jnp.bfloat16)
    x_pair.wait_recv()
    xt[:, length:] = jnp.transpose(xsib[...]).astype(jnp.bfloat16)

    ext[core] = jnp.zeros_like(tot)
    for j in range(1, chips):
        kind = 1 - (chip - j + chips) // chips
        states[j - 1].wait_recv()
        ext[core, kind] += srecv[j - 1]
    share = remote(ext.at[core], ext.at[core], e_send, e_recv, {"ctx": sibling})
    share_in = remote(ext.at[1 - core], ext.at[1 - core], e_send, e_recv, {"ctx": sibling})
    share.start()
    pair_rest = remote(st.at[1 - core], sib.at[1 - core], p_send.at[1], p_recv.at[1], {"ctx": sibling})
    pair_rest.wait_recv()
    share_in.wait_recv()

    second = core.astype(jnp.float32)
    first = 1.0 - second

    def suffix(h):
        a, i = h // half, h % half
        return (scale * (ext[a, 1, i] + first * sib[a, 1, i])).astype(jnp.bfloat16)

    def prefix(h):
        a, i = h // half, h % half
        return (scale * (ext[a, 0, i] + second * sib[a, 0, i])).astype(jnp.bfloat16)

    for h in range(heads):
        out = acc[2, :, cols(h)] + dot(k[:, cols(h)], suffix(h), NN)
        dv[:, cols(h)] = out.astype(jnp.bfloat16)
    for j in range(n):
        dvs[j % 2, j // 2] = dv[:, j * cb:(j + 1) * cb].astype(jnp.float32)
    value = remote(dvs.at[1 - core], dvr, d_send, d_recv, {"ctx": sibling})
    value.start()
    value.wait_recv()

    for mask in range(chips - 1, -1, -1):
        to = flip(mask)
        both = jnp.concatenate([dvs[core, to], dvr[to]], 0).astype(jnp.bfloat16)
        tile = dot(xt[...], both, NN)
        for d in range(m):
            for s in range(2):
                lo = d * rows + s * part
                wt[s, d, place(s, mask)] = tile[lo:lo + part]

    def chunk(c):
        return lax.rem(row + c + 1, m)

    def halve(s, c, i):
        lo = 1 << (bits - 1 - i)
        d = chunk(c)
        return remote(
            wt.at[s, d, pl.ds(lo, lo)], wr.at[s, d, pl.ds(lo, lo)],
            r_send.at[s, c, i], r_recv.at[s, c, i], {"ctx": flip(1 << orders[s][i]) * 2 + core},
        )

    def across(s, c):
        return remote(
            wt.at[s, chunk(c), 0], wrecv.at[s, c], w_send.at[s, c], w_recv.at[s, c],
            {"dp": chunk(c)},
        )

    def advance(s, c, i):
        d = chunk(c)
        if i > 0:
            lo = 1 << (bits - i)
            halve(s, c, i - 1).wait_recv()
            wt[s, d, 0:lo] += wr[s, d, lo:2 * lo]
        if i < bits:
            halve(s, c, i).start()
        elif c < m - 1:
            across(s, c).start()

    def step(t):
        for i in range(bits + 1):
            for s in range(2):
                if 0 <= t - i < m:
                    advance(s, t - i, i)

    for s in range(2):
        advance(s, 0, 0)

    for h in range(heads):
        out = acc[0, :, cols(h)] + dot(g[:, cols(h)], prefix(h), NT)
        dq[:, cols(h)] = out.astype(jnp.bfloat16)
        out = acc[1, :, cols(h)] + dot(v[:, cols(h)], suffix(h), NT)
        dk[:, cols(h)] = out.astype(jnp.bfloat16)

    for t in range(1, m + bits):
        step(t)
    for s in range(2):
        out = wt[s, row, 0]
        for c in range(m - 1):
            across(s, c).wait_recv()
            out = out + wrecv[s, c]
        w[s * part:(s + 1) * part] = out * rscale

    for c in pair + states + [x_pair, share, value]:
        c.wait_send()
    for s in range(2):
        for c in range(m):
            for i in range(bits):
                halve(s, c, i).wait_send()
            if c < m - 1:
                across(s, c).wait_send()


def copy_out(*refs):
    count = len(refs) // 2
    sems = refs[-1]
    copies = [pltpu.make_async_copy(refs[i], refs[count + i], sems.at[i]) for i in range(count)]
    for c in copies:
        c.start()
    for c in copies:
        c.wait()


def on_device(query_heads, key_heads, value_heads, grad_output, layer_input):
    length, width = query_heads.shape[1:]
    wide = layer_input.shape[2]
    n = lax.axis_size("ctx")
    m = lax.axis_size("dp")
    scale = 1.0 / math.sqrt(HD * length * n)
    rscale = 1.0 / math.sqrt(m * length * n)
    heads, chips, cb, rows = width // HD, n // 2, width // n, wide // m
    half, bits = heads // 2, chips.bit_length() - 1
    f32, bf16 = jnp.float32, jnp.bfloat16
    vmem = pl.BlockSpec(memory_space=pltpu.VMEM)
    dma = pltpu.SemaphoreType.DMA
    out = jax.ShapeDtypeStruct((length, width), bf16)
    dq, dk, dv, w = pl.pallas_call(
        functools.partial(kernel, n, m, scale, rscale),
        out_shape=(out, out, out, jax.ShapeDtypeStruct((rows, cb), f32)),
        in_specs=[vmem] * 5,
        out_specs=(vmem,) * 4,
        scratch_shapes=[
            pltpu.VMEM((length, wide), f32),
            pltpu.VMEM((length, wide), f32),
            pltpu.VMEM((wide, 2 * length), bf16),
            pltpu.VMEM((2, 2, half, HD, HD), f32),
            pltpu.VMEM((2, 2, half, HD, HD), f32),
            pltpu.VMEM((2, half, HD, HD), f32),
            pltpu.VMEM((max(chips - 1, 1), half, HD, HD), f32),
            pltpu.VMEM((2, 2, half, HD, HD), f32),
            pltpu.VMEM((3, length, width), f32),
            pltpu.VMEM((2, chips, length, cb), f32),
            pltpu.VMEM((chips, length, cb), f32),
            pltpu.VMEM((2, m, chips, rows // 2, cb), f32),
            pltpu.VMEM((2, m, chips, rows // 2, cb), f32),
            pltpu.VMEM((2, max(m - 1, 1), rows // 2, cb), f32),
            dma, dma,
            dma((2,)), dma((2,)),
            dma((max(chips - 1, 1),)), dma((max(chips - 1, 1),)),
            dma, dma,
            dma, dma,
            dma((2, m, max(bits, 1))), dma((2, m, max(bits, 1))),
            dma((2, max(m - 1, 1))), dma((2, max(m - 1, 1))),
        ],
        compiler_params=pltpu.CompilerParams(
            collective_id=0, has_side_effects=True, vmem_limit_bytes=56 * 2**20
        ),
    )(query_heads[0], key_heads[0], value_heads[0], grad_output[0], layer_input[0])
    made = (dq, dk, dv, w)
    dq, dk, dv, w = pl.pallas_call(
        copy_out,
        out_shape=tuple(jax.ShapeDtypeStruct(r.shape, r.dtype) for r in made),
        in_specs=[pl.BlockSpec(memory_space=pltpu.HBM)] * len(made),
        out_specs=(pl.BlockSpec(memory_space=pltpu.HBM),) * len(made),
        scratch_shapes=[dma((len(made),))],
    )(*made)
    return dq[None], dk[None], dv[None], w


def solution(mesh):
    spec = P("dp", "ctx", None)
    return jax.shard_map(
        on_device, mesh=mesh, in_specs=(spec,) * 5,
        out_specs=(spec, spec, spec, P("dp", "ctx")), check_vma=False,
    )
```

```python
import functools
import math

import jax
import jax.numpy as jnp
from jax import lax
from jax.experimental import pallas as pl
from jax.experimental.pallas import tpu as pltpu
from jax.sharding import PartitionSpec as P

HD = 128
NN = (((1,), (0,)), ((), ()))
NT = (((1,), (1,)), ((), ()))
TN = (((0,), (0,)), ((), ()))


def dot(a, b, dims):
    return lax.dot_general(a, b, dims, preferred_element_type=jnp.float32)


def kernel(
    n, m, scale, rscale,
    q, k, v, g, x,
    dq, dk, dv, w,
    xs, xsib, xt, st, sib, tot, srecv, ext, acc, dvs, dvr, wt, wr, wrecv,
    x_send, x_recv, p_send, p_recv, s_send, s_recv, e_send, e_recv,
    d_send, d_recv, r_send, r_recv, w_send, w_recv,
):
    length, width = q.shape
    heads = width // HD
    half = heads // 2
    chips = n // 2
    cb = dvs.shape[3]
    rows = w.shape[0]
    part = rows // 2
    bits = chips.bit_length() - 1
    me = lax.axis_index("ctx")
    row = lax.axis_index("dp")
    core = lax.rem(me, 2)
    chip = me // 2
    sibling = me + 1 - 2 * core

    def flip(mask):
        out = chip
        for b in range(bits):
            if mask >> b & 1:
                out = out + (1 << b) * (1 - 2 * lax.rem(chip // (1 << b), 2))
        return out

    def remote(src, dst, send, recv, to):
        return pltpu.make_async_remote_copy(
            src_ref=src, dst_ref=dst, send_sem=send, recv_sem=recv,
            device_id=to, device_id_type=pl.DeviceIdType.MESH,
        )

    orders = ([*range(bits)], [*range(bits - 1, -1, -1)])

    def place(s, mask):
        return sum((mask >> b & 1) << (bits - 1 - i) for i, b in enumerate(orders[s]))

    barrier = pltpu.get_barrier_semaphore()
    for j in range(1, n):
        pl.semaphore_signal(
            barrier, inc=1, device_id={"ctx": lax.rem(me + j, n)},
            device_id_type=pl.DeviceIdType.MESH,
        )
    for j in range(1, m):
        pl.semaphore_signal(
            barrier, inc=1, device_id={"dp": lax.rem(row + j, m)},
            device_id_type=pl.DeviceIdType.MESH,
        )

    def cols(h):
        return slice(h * HD, (h + 1) * HD)

    for h in range(heads):
        a, i = h // half, h % half
        st[a, 0, i] = dot(k[:, cols(h)], v[:, cols(h)], TN)
        st[a, 1, i] = dot(q[:, cols(h)], g[:, cols(h)], TN)
    xs[...] = x[...].astype(jnp.float32)
    pl.semaphore_wait(barrier, n - 1 + m - 1)

    pair = [
        remote(st.at[1 - core], sib.at[1 - core], p_send.at[0], p_recv.at[0], {"ctx": sibling}),
        remote(st.at[core], sib.at[core], p_send.at[1], p_recv.at[1], {"ctx": sibling}),
    ]
    pair_in = remote(st.at[core], sib.at[core], p_send.at[0], p_recv.at[0], {"ctx": sibling})
    for c in pair:
        c.start()
    x_pair = remote(xs, xsib, x_send, x_recv, {"ctx": sibling})
    pair_in.wait_recv()
    tot[...] = st[core] + sib[core]
    states = []
    for j in range(1, chips):
        wrap = (chip + j) // chips
        to = (chip + j - chips * wrap) * 2 + core
        c = remote(tot.at[wrap], srecv.at[j - 1], s_send.at[j - 1], s_recv.at[j - 1], {"ctx": to})
        c.start()
        states.append(c)
    x_pair.start()

    at_row = lax.broadcasted_iota(jnp.int32, (length, length), 0)
    at_col = lax.broadcasted_iota(jnp.int32, (length, length), 1)
    lower = at_row >= at_col
    upper = at_row <= at_col
    for h in range(heads):
        qh, kh, vh, gh = (r[:, cols(h)] for r in (q, k, v, g))
        score_t = jnp.where(upper, scale * dot(kh, qh, NT), 0.0).astype(jnp.bfloat16)
        grad = jnp.where(lower, scale * dot(gh, vh, NT), 0.0).astype(jnp.bfloat16)
        acc[0, :, cols(h)] = dot(grad, kh, NN)
        acc[1, :, cols(h)] = dot(grad, qh, TN)
        acc[2, :, cols(h)] = dot(score_t, gh, NN)

    xt[:, :length] = jnp.transpose(xs[...]).astype(jnp.bfloat16)
    x_pair.wait_recv()
    xt[:, length:] = jnp.transpose(xsib[...]).astype(jnp.bfloat16)

    ext[core] = jnp.zeros_like(tot)
    for j in range(1, chips):
        kind = 1 - (chip - j + chips) // chips
        states[j - 1].wait_recv()
        ext[core, kind] += srecv[j - 1]
    share = remote(ext.at[core], ext.at[core], e_send, e_recv, {"ctx": sibling})
    share_in = remote(ext.at[1 - core], ext.at[1 - core], e_send, e_recv, {"ctx": sibling})
    share.start()
    pair_rest = remote(st.at[1 - core], sib.at[1 - core], p_send.at[1], p_recv.at[1], {"ctx": sibling})
    pair_rest.wait_recv()
    share_in.wait_recv()

    second = core.astype(jnp.float32)
    first = 1.0 - second

    def suffix(h):
        a, i = h // half, h % half
        return (scale * (ext[a, 1, i] + first * sib[a, 1, i])).astype(jnp.bfloat16)

    def prefix(h):
        a, i = h // half, h % half
        return (scale * (ext[a, 0, i] + second * sib[a, 0, i])).astype(jnp.bfloat16)

    for h in range(heads):
        out = acc[2, :, cols(h)] + dot(k[:, cols(h)], suffix(h), NN)
        dv[:, cols(h)] = out.astype(jnp.bfloat16)
    for j in range(n):
        dvs[j % 2, j // 2] = dv[:, j * cb:(j + 1) * cb].astype(jnp.float32)
    value = remote(dvs.at[1 - core], dvr, d_send, d_recv, {"ctx": sibling})
    value.start()
    value.wait_recv()

    for mask in range(chips - 1, -1, -1):
        to = flip(mask)
        both = jnp.concatenate([dvs[core, to], dvr[to]], 0).astype(jnp.bfloat16)
        tile = dot(xt[...], both, NN)
        for d in range(m):
            for s in range(2):
                lo = d * rows + s * part
                wt[s, d, place(s, mask)] = tile[lo:lo + part]

    def chunk(c):
        return lax.rem(row + c + 1, m)

    def halve(s, c, i):
        lo = 1 << (bits - 1 - i)
        d = chunk(c)
        return remote(
            wt.at[s, d, pl.ds(lo, lo)], wr.at[s, d, pl.ds(lo, lo)],
            r_send.at[s, c, i], r_recv.at[s, c, i], {"ctx": flip(1 << orders[s][i]) * 2 + core},
        )

    def across(s, c):
        return remote(
            wt.at[s, chunk(c), 0], wrecv.at[s, c], w_send.at[s, c], w_recv.at[s, c],
            {"dp": chunk(c)},
        )

    def advance(s, c, i):
        d = chunk(c)
        if i > 0:
            lo = 1 << (bits - i)
            halve(s, c, i - 1).wait_recv()
            wt[s, d, 0:lo] += wr[s, d, lo:2 * lo]
        if i < bits:
            halve(s, c, i).start()
        elif c < m - 1:
            across(s, c).start()

    def step(t):
        for i in range(bits + 1):
            for s in range(2):
                if 0 <= t - i < m:
                    advance(s, t - i, i)

    for s in range(2):
        advance(s, 0, 0)

    for h in range(heads):
        out = acc[0, :, cols(h)] + dot(g[:, cols(h)], prefix(h), NT)
        dq[:, cols(h)] = out.astype(jnp.bfloat16)
        out = acc[1, :, cols(h)] + dot(v[:, cols(h)], suffix(h), NT)
        dk[:, cols(h)] = out.astype(jnp.bfloat16)

    for t in range(1, m + bits):
        step(t)
    for s in range(2):
        out = wt[s, row, 0]
        for c in range(m - 1):
            across(s, c).wait_recv()
            out = out + wrecv[s, c]
        w[s * part:(s + 1) * part] = out * rscale

    for c in pair + states + [x_pair, share, value]:
        c.wait_send()
    for s in range(2):
        for c in range(m):
            for i in range(bits):
                halve(s, c, i).wait_send()
            if c < m - 1:
                across(s, c).wait_send()


def copy_out(*refs):
    count = (len(refs) - 1) // 3
    sems = refs[-1]

    def copies(source, target, at):
        return [
            pltpu.make_async_copy(refs[source * count + i], refs[target * count + i], sems.at[at, i])
            for i in range(count)
        ]

    into, out = copies(0, 2, 0), copies(2, 1, 1)
    for c in into:
        c.start()
    for i in range(count):
        into[i].wait()
        out[i].start()
    for c in out:
        c.wait()


def on_device(query_heads, key_heads, value_heads, grad_output, layer_input):
    length, width = query_heads.shape[1:]
    wide = layer_input.shape[2]
    n = lax.axis_size("ctx")
    m = lax.axis_size("dp")
    scale = 1.0 / math.sqrt(HD * length * n)
    rscale = 1.0 / math.sqrt(m * length * n)
    heads, chips, cb, rows = width // HD, n // 2, width // n, wide // m
    half, bits = heads // 2, chips.bit_length() - 1
    f32, bf16 = jnp.float32, jnp.bfloat16
    vmem = pl.BlockSpec(memory_space=pltpu.VMEM)
    dma = pltpu.SemaphoreType.DMA
    out = jax.ShapeDtypeStruct((length, width), bf16)
    dq, dk, dv, w = pl.pallas_call(
        functools.partial(kernel, n, m, scale, rscale),
        out_shape=(out, out, out, jax.ShapeDtypeStruct((rows, cb), f32)),
        in_specs=[vmem] * 5,
        out_specs=(vmem,) * 4,
        scratch_shapes=[
            pltpu.VMEM((length, wide), f32),
            pltpu.VMEM((length, wide), f32),
            pltpu.VMEM((wide, 2 * length), bf16),
            pltpu.VMEM((2, 2, half, HD, HD), f32),
            pltpu.VMEM((2, 2, half, HD, HD), f32),
            pltpu.VMEM((2, half, HD, HD), f32),
            pltpu.VMEM((max(chips - 1, 1), half, HD, HD), f32),
            pltpu.VMEM((2, 2, half, HD, HD), f32),
            pltpu.VMEM((3, length, width), f32),
            pltpu.VMEM((2, chips, length, cb), f32),
            pltpu.VMEM((chips, length, cb), f32),
            pltpu.VMEM((2, m, chips, rows // 2, cb), f32),
            pltpu.VMEM((2, m, chips, rows // 2, cb), f32),
            pltpu.VMEM((2, max(m - 1, 1), rows // 2, cb), f32),
            dma, dma,
            dma((2,)), dma((2,)),
            dma((max(chips - 1, 1),)), dma((max(chips - 1, 1),)),
            dma, dma,
            dma, dma,
            dma((2, m, max(bits, 1))), dma((2, m, max(bits, 1))),
            dma((2, max(m - 1, 1))), dma((2, max(m - 1, 1))),
        ],
        compiler_params=pltpu.CompilerParams(
            collective_id=0, has_side_effects=True, vmem_limit_bytes=56 * 2**20
        ),
    )(query_heads[0], key_heads[0], value_heads[0], grad_output[0], layer_input[0])
    made = (dq, dk, dv, w)
    dq, dk, dv, w = pl.pallas_call(
        copy_out,
        out_shape=tuple(jax.ShapeDtypeStruct(r.shape, r.dtype) for r in made),
        in_specs=[pl.BlockSpec(memory_space=pltpu.HBM)] * len(made),
        out_specs=(pl.BlockSpec(memory_space=pltpu.HBM),) * len(made),
        scratch_shapes=[pltpu.VMEM(r.shape, r.dtype) for r in made] + [dma((2, len(made)))],
    )(*made)
    return dq[None], dk[None], dv[None], w


def solution(mesh):
    spec = P("dp", "ctx", None)
    return jax.shard_map(
        on_device, mesh=mesh, in_specs=(spec,) * 5,
        out_specs=(spec, spec, spec, P("dp", "ctx")), check_vma=False,
    )
```

```python
import functools
import math

import jax
import jax.numpy as jnp
from jax import lax
from jax.experimental import pallas as pl
from jax.experimental.pallas import tpu as pltpu
from jax.sharding import PartitionSpec as P

HD = 128
NN = (((1,), (0,)), ((), ()))
NT = (((1,), (1,)), ((), ()))
TN = (((0,), (0,)), ((), ()))


def dot(a, b, dims):
    return lax.dot_general(a, b, dims, preferred_element_type=jnp.float32)


def kernel(
    n, m, scale, rscale,
    q, k, v, g, x,
    dq, dk, dv, w,
    xs, xsib, xt, st, sib, tot, srecv, ext, acc, gw, dvs, dvr, wt, wr, wrecv,
    x_send, x_recv, p_send, p_recv, s_send, s_recv, e_send, e_recv,
    d_send, d_recv, r_send, r_recv, w_send, w_recv,
):
    length, width = q.shape
    heads = width // HD
    half = heads // 2
    chips = n // 2
    cb = dvs.shape[3]
    rows = w.shape[0]
    part = rows // 2
    bits = chips.bit_length() - 1
    me = lax.axis_index("ctx")
    row = lax.axis_index("dp")
    core = lax.rem(me, 2)
    chip = me // 2
    sibling = me + 1 - 2 * core

    def flip(mask):
        out = chip
        for b in range(bits):
            if mask >> b & 1:
                out = out + (1 << b) * (1 - 2 * lax.rem(chip // (1 << b), 2))
        return out

    def remote(src, dst, send, recv, to):
        return pltpu.make_async_remote_copy(
            src_ref=src, dst_ref=dst, send_sem=send, recv_sem=recv,
            device_id=to, device_id_type=pl.DeviceIdType.MESH,
        )

    orders = ([*range(bits)], [*range(bits - 1, -1, -1)])

    def place(s, mask):
        return sum((mask >> b & 1) << (bits - 1 - i) for i, b in enumerate(orders[s]))

    barrier = pltpu.get_barrier_semaphore()
    for j in range(1, n):
        pl.semaphore_signal(
            barrier, inc=1, device_id={"ctx": lax.rem(me + j, n)},
            device_id_type=pl.DeviceIdType.MESH,
        )
    for j in range(1, m):
        pl.semaphore_signal(
            barrier, inc=1, device_id={"dp": lax.rem(row + j, m)},
            device_id_type=pl.DeviceIdType.MESH,
        )

    def cols(h):
        return slice(h * HD, (h + 1) * HD)

    def blocks(kind, left, right):
        for h in range(heads):
            st[h // half, kind, h % half] = dot(left[:, cols(h)], right[:, cols(h)], TN)

    blocks(1, q, g)
    xs[...] = x[...].astype(jnp.float32)
    pl.semaphore_wait(barrier, n - 1 + m - 1)

    def pair(a, kind, at):
        return remote(st.at[a, kind], sib.at[a, kind], p_send.at[at], p_recv.at[at], {"ctx": sibling})

    pairs = [pair(1 - core, 1, 0), pair(1 - core, 0, 1), pair(core, 1, 2), pair(core, 0, 3)]
    pairs_in = [pair(core, 1, 0), pair(core, 0, 1), pair(1 - core, 1, 2), pair(1 - core, 0, 3)]
    x_pair = remote(xs, xsib, x_send, x_recv, {"ctx": sibling})
    pairs[0].start()
    blocks(0, k, v)

    def bit(i):
        return lax.rem(chip // (1 << i), 2)

    def sends(kind, i):
        above = chip // (1 << (i + 1))
        if kind:
            return (bit(i) == 1) | (above != 0)
        return (bit(i) == 0) | (above != (chips >> (i + 1)) - 1)

    def takes(kind, i):
        above = chip // (1 << (i + 1))
        if kind:
            return (bit(i) == 0) | (above != 0)
        return (bit(i) == 1) | (above != (chips >> (i + 1)) - 1)

    def scan_copy(kind, i, c):
        return remote(
            tot.at[kind, i, c], srecv.at[kind, i, c],
            s_send.at[kind, i, c], s_recv.at[kind, i, c], {"ctx": flip(1 << i) * 2 + core},
        )

    def scan_send(kind, i, c):
        @pl.when(sends(kind, i))
        def _():
            scan_copy(kind, i, c).start()

    def scan_take(kind, i, c):
        @pl.when(takes(kind, i))
        def _():
            scan_copy(kind, i, c).wait_recv()

            @pl.when(bit(i) == 1 - kind)
            def _():
                ext[core, kind, c] += srecv[kind, i, c]

            if i < bits - 1:
                tot[kind, i + 1, c] = tot[kind, i, c] + srecv[kind, i, c]

        if i < bits - 1:
            scan_send(kind, i + 1, c)

    def scan_begin(kind):
        pairs_in[1 - kind].wait_recv()
        for c in range(half):
            tot[kind, 0, c] = st[core, kind, c] + sib[core, kind, c]
            if bits > 0:
                scan_send(kind, 0, c)

    def share(a, kind):
        return remote(ext.at[a, kind], ext.at[a, kind], e_send.at[kind], e_recv.at[kind], {"ctx": sibling})

    ext[core] = jnp.zeros((2, half, HD, HD), jnp.float32)
    scan_begin(1)
    for c in pairs[1:]:
        c.start()
    x_pair.start()

    at_row = lax.broadcasted_iota(jnp.int32, (length, length), 0)
    at_col = lax.broadcasted_iota(jnp.int32, (length, length), 1)
    lower = at_row >= at_col
    upper = at_row <= at_col

    def value_inside(heads_now):
        for h in heads_now:
            score_t = jnp.where(upper, scale * dot(k[:, cols(h)], q[:, cols(h)], NT), 0.0)
            acc[:, cols(h)] = dot(score_t.astype(jnp.bfloat16), g[:, cols(h)], NN)

    value_inside(range(half))
    xt[:, :length] = jnp.transpose(xs[...]).astype(jnp.bfloat16)
    if bits > 0:
        for c in range(half):
            scan_take(1, 0, c)
    scan_begin(0)
    value_inside(range(half, heads))
    x_pair.wait_recv()
    xt[:, length:] = jnp.transpose(xsib[...]).astype(jnp.bfloat16)
    for i in range(1, bits):
        for c in range(half):
            scan_take(1, i, c)
    share(core, 1).start()
    pairs_in[2].wait_recv()
    share(1 - core, 1).wait_recv()

    second = core.astype(jnp.float32)
    first = 1.0 - second

    def suffix(h):
        a, i = h // half, h % half
        return (scale * (ext[a, 1, i] + first * sib[a, 1, i])).astype(jnp.bfloat16)

    def prefix(h):
        a, i = h // half, h % half
        return (scale * (ext[a, 0, i] + second * sib[a, 0, i])).astype(jnp.bfloat16)

    for h in range(heads):
        out = acc[:, cols(h)] + dot(k[:, cols(h)], suffix(h), NN)
        dv[:, cols(h)] = out.astype(jnp.bfloat16)
    for j in range(n):
        dvs[j % 2, j // 2] = dv[:, j * cb:(j + 1) * cb].astype(jnp.float32)
    value = remote(dvs.at[1 - core], dvr, d_send, d_recv, {"ctx": sibling})
    value.start()
    if bits > 0:
        for c in range(half):
            scan_take(0, 0, c)
    value.wait_recv()

    def chunk(c):
        return lax.rem(row + c + 1, m)

    def halve(s, c, i):
        lo = 1 << (bits - 1 - i)
        d = chunk(c)
        return remote(
            wt.at[s, d, pl.ds(lo, lo)], wr.at[s, d, pl.ds(lo, lo)],
            r_send.at[s, c, i], r_recv.at[s, c, i], {"ctx": flip(1 << orders[s][i]) * 2 + core},
        )

    def across(s, c):
        return remote(
            wt.at[s, chunk(c), 0], wrecv.at[s, c], w_send.at[s, c], w_recv.at[s, c],
            {"dp": chunk(c)},
        )

    def advance(s, c, i):
        d = chunk(c)
        if i > 0:
            lo = 1 << (bits - i)
            halve(s, c, i - 1).wait_recv()
            wt[s, d, 0:lo] += wr[s, d, lo:2 * lo]
        if i < bits:
            halve(s, c, i).start()
        elif c < m - 1:
            across(s, c).start()

    for mask in range(chips - 1, -1, -1):
        to = flip(mask)
        both = jnp.concatenate([dvs[core, to], dvr[to]], 0).astype(jnp.bfloat16)
        tile = dot(xt[...], both, NN)
        for d in range(m):
            for s in range(2):
                lo = d * rows + s * part
                wt[s, d, place(s, mask)] = tile[lo:lo + part]
        for s in range(2):
            if bits > 0 and mask == 1 << orders[s][0]:
                advance(s, 0, 0)

    def key_out(heads_now):
        for h in heads_now:
            grad = jnp.where(lower, scale * dot(g[:, cols(h)], v[:, cols(h)], NT), 0.0)
            gw[h] = grad.astype(jnp.bfloat16)
            out = dot(gw[h], q[:, cols(h)], TN) + dot(v[:, cols(h)], suffix(h), NT)
            dk[:, cols(h)] = out.astype(jnp.bfloat16)

    def prefix_in():
        for i in range(1, bits):
            for c in range(half):
                scan_take(0, i, c)
        share(core, 0).start()

    def query_out(heads_now):
        for h in heads_now:
            out = dot(gw[h], k[:, cols(h)], NN) + dot(g[:, cols(h)], prefix(h), NT)
            dq[:, cols(h)] = out.astype(jnp.bfloat16)

    def prefix_done():
        pairs_in[3].wait_recv()
        share(1 - core, 0).wait_recv()
        query_out(range(half))

    pieces = [
        lambda: key_out(range(half)),
        lambda: (prefix_in(), key_out(range(half, heads))),
        prefix_done,
        lambda: query_out(range(half, heads)),
    ]
    if bits == 0:
        for s in range(2):
            advance(s, 0, 0)
    for t in range(1, m + bits):
        for i in range(bits + 1):
            for s in range(2):
                if 0 <= t - i < m:
                    advance(s, t - i, i)
            if i == 0 and pieces:
                pieces.pop(0)()
    for piece in pieces:
        piece()
    for s in range(2):
        out = wt[s, row, 0]
        for c in range(m - 1):
            across(s, c).wait_recv()
            out = out + wrecv[s, c]
        w[s * part:(s + 1) * part] = out * rscale

    for c in pairs + [x_pair, share(core, 0), share(core, 1), value]:
        c.wait_send()
    for kind in range(2):
        for i in range(bits):
            @pl.when(sends(kind, i))
            def _():
                for c in range(half):
                    scan_copy(kind, i, c).wait_send()
    for s in range(2):
        for c in range(m):
            for i in range(bits):
                halve(s, c, i).wait_send()
            if c < m - 1:
                across(s, c).wait_send()


def copy_out(*refs):
    count = (len(refs) - 1) // 3
    sems = refs[-1]

    def copies(source, target, at):
        return [
            pltpu.make_async_copy(refs[source * count + i], refs[target * count + i], sems.at[at, i])
            for i in range(count)
        ]

    into, out = copies(0, 2, 0), copies(2, 1, 1)
    for c in into:
        c.start()
    for i in range(count):
        into[i].wait()
        out[i].start()
    for c in out:
        c.wait()


def on_device(query_heads, key_heads, value_heads, grad_output, layer_input):
    length, width = query_heads.shape[1:]
    wide = layer_input.shape[2]
    n = lax.axis_size("ctx")
    m = lax.axis_size("dp")
    scale = 1.0 / math.sqrt(HD * length * n)
    rscale = 1.0 / math.sqrt(m * length * n)
    heads, chips, cb, rows = width // HD, n // 2, width // n, wide // m
    half, bits = heads // 2, chips.bit_length() - 1
    f32, bf16 = jnp.float32, jnp.bfloat16
    vmem = pl.BlockSpec(memory_space=pltpu.VMEM)
    dma = pltpu.SemaphoreType.DMA
    out = jax.ShapeDtypeStruct((length, width), bf16)
    dq, dk, dv, w = pl.pallas_call(
        functools.partial(kernel, n, m, scale, rscale),
        out_shape=(out, out, out, jax.ShapeDtypeStruct((rows, cb), f32)),
        in_specs=[vmem] * 5,
        out_specs=(vmem,) * 4,
        scratch_shapes=[
            pltpu.VMEM((length, wide), f32),
            pltpu.VMEM((length, wide), f32),
            pltpu.VMEM((wide, 2 * length), bf16),
            pltpu.VMEM((2, 2, half, HD, HD), f32),
            pltpu.VMEM((2, 2, half, HD, HD), f32),
            pltpu.VMEM((2, max(bits, 1), half, HD, HD), f32),
            pltpu.VMEM((2, max(bits, 1), half, HD, HD), f32),
            pltpu.VMEM((2, 2, half, HD, HD), f32),
            pltpu.VMEM((length, width), f32),
            pltpu.VMEM((heads, length, length), bf16),
            pltpu.VMEM((2, chips, length, cb), f32),
            pltpu.VMEM((chips, length, cb), f32),
            pltpu.VMEM((2, m, chips, rows // 2, cb), f32),
            pltpu.VMEM((2, m, chips, rows // 2, cb), f32),
            pltpu.VMEM((2, max(m - 1, 1), rows // 2, cb), f32),
            dma, dma,
            dma((4,)), dma((4,)),
            dma((2, max(bits, 1), half)), dma((2, max(bits, 1), half)),
            dma((2,)), dma((2,)),
            dma, dma,
            dma((2, m, max(bits, 1))), dma((2, m, max(bits, 1))),
            dma((2, max(m - 1, 1))), dma((2, max(m - 1, 1))),
        ],
        compiler_params=pltpu.CompilerParams(
            collective_id=0, has_side_effects=True, vmem_limit_bytes=56 * 2**20
        ),
    )(query_heads[0], key_heads[0], value_heads[0], grad_output[0], layer_input[0])
    made = (dq, dk, dv, w)
    dq, dk, dv, w = pl.pallas_call(
        copy_out,
        out_shape=tuple(jax.ShapeDtypeStruct(r.shape, r.dtype) for r in made),
        in_specs=[pl.BlockSpec(memory_space=pltpu.HBM)] * len(made),
        out_specs=(pl.BlockSpec(memory_space=pltpu.HBM),) * len(made),
        scratch_shapes=[pltpu.VMEM(r.shape, r.dtype) for r in made] + [dma((2, len(made)))],
    )(*made)
    return dq[None], dk[None], dv[None], w


def solution(mesh):
    spec = P("dp", "ctx", None)
    return jax.shard_map(
        on_device, mesh=mesh, in_specs=(spec,) * 5,
        out_specs=(spec, spec, spec, P("dp", "ctx")), check_vma=False,
    )
```

```python
import functools
import math

import jax
import jax.numpy as jnp
from jax import lax
from jax.experimental import pallas as pl
from jax.experimental.pallas import tpu as pltpu
from jax.sharding import PartitionSpec as P

HD = 128
NN = (((1,), (0,)), ((), ()))
NT = (((1,), (1,)), ((), ()))
TN = (((0,), (0,)), ((), ()))


def dot(a, b, dims):
    return lax.dot_general(a, b, dims, preferred_element_type=jnp.float32)


def kernel(
    n, m, scale, rscale,
    q, k, v, g, x,
    dq, dk, dv, w,
    xs, xsib, xt, st, sib, tot, srecv, ext, acc, gw, dvs, dvr, wt, wr, wrecv,
    x_send, x_recv, p_send, p_recv, s_send, s_recv, e_send, e_recv,
    d_send, d_recv, r_send, r_recv, w_send, w_recv,
):
    length, width = q.shape
    heads = width // HD
    half = heads // 2
    chips = n // 2
    cb = dvs.shape[3]
    rows = w.shape[0]
    part = rows // 2
    bits = chips.bit_length() - 1
    me = lax.axis_index("ctx")
    row = lax.axis_index("dp")
    core = lax.rem(me, 2)
    chip = me // 2
    sibling = me + 1 - 2 * core

    def flip(mask):
        out = chip
        for b in range(bits):
            if mask >> b & 1:
                out = out + (1 << b) * (1 - 2 * lax.rem(chip // (1 << b), 2))
        return out

    def remote(src, dst, send, recv, to):
        return pltpu.make_async_remote_copy(
            src_ref=src, dst_ref=dst, send_sem=send, recv_sem=recv,
            device_id=to, device_id_type=pl.DeviceIdType.MESH,
        )

    orders = ([*range(bits)], [*range(bits - 1, -1, -1)])

    def place(s, mask):
        return sum((mask >> b & 1) << (bits - 1 - i) for i, b in enumerate(orders[s]))

    barrier = pltpu.get_barrier_semaphore()
    for j in range(1, n):
        pl.semaphore_signal(
            barrier, inc=1, device_id={"ctx": lax.rem(me + j, n)},
            device_id_type=pl.DeviceIdType.MESH,
        )
    for j in range(1, m):
        pl.semaphore_signal(
            barrier, inc=1, device_id={"dp": lax.rem(row + j, m)},
            device_id_type=pl.DeviceIdType.MESH,
        )

    def cols(h):
        return slice(h * HD, (h + 1) * HD)

    def blocks(kind, left, right):
        for h in range(heads):
            st[h // half, kind, h % half] = dot(left[:, cols(h)], right[:, cols(h)], TN)

    blocks(1, q, g)
    xs[...] = x[...].astype(jnp.float32)
    pl.semaphore_wait(barrier, n - 1 + m - 1)

    def pair(a, kind, at):
        return remote(st.at[a, kind], sib.at[a, kind], p_send.at[at], p_recv.at[at], {"ctx": sibling})

    pairs = [pair(1 - core, 1, 0), pair(1 - core, 0, 1), pair(core, 1, 2), pair(core, 0, 3)]
    pairs_in = [pair(core, 1, 0), pair(core, 0, 1), pair(1 - core, 1, 2), pair(1 - core, 0, 3)]
    x_pair = remote(xs, xsib, x_send, x_recv, {"ctx": sibling})
    pairs[0].start()
    blocks(0, k, v)

    def bit(i):
        return lax.rem(chip // (1 << i), 2)

    def sends(kind, i):
        above = chip // (1 << (i + 1))
        if kind:
            return (bit(i) == 1) | (above != 0)
        return (bit(i) == 0) | (above != (chips >> (i + 1)) - 1)

    def takes(kind, i):
        above = chip // (1 << (i + 1))
        if kind:
            return (bit(i) == 0) | (above != 0)
        return (bit(i) == 1) | (above != (chips >> (i + 1)) - 1)

    def scan_copy(kind, i, c):
        return remote(
            tot.at[kind, i, c], srecv.at[kind, i, c],
            s_send.at[kind, i, c], s_recv.at[kind, i, c], {"ctx": flip(1 << i) * 2 + core},
        )

    def scan_send(kind, i, c):
        @pl.when(sends(kind, i))
        def _():
            scan_copy(kind, i, c).start()

    def scan_take(kind, i, c):
        @pl.when(takes(kind, i))
        def _():
            scan_copy(kind, i, c).wait_recv()

            @pl.when(bit(i) == 1 - kind)
            def _():
                ext[core, kind, c] += srecv[kind, i, c]

            if i < bits - 1:
                tot[kind, i + 1, c] = tot[kind, i, c] + srecv[kind, i, c]

        if i < bits - 1:
            scan_send(kind, i + 1, c)

    def scan_begin(kind):
        pairs_in[1 - kind].wait_recv()
        for c in range(half):
            tot[kind, 0, c] = st[core, kind, c] + sib[core, kind, c]
            if bits > 0:
                scan_send(kind, 0, c)

    def share(a, kind):
        return remote(ext.at[a, kind], ext.at[a, kind], e_send.at[kind], e_recv.at[kind], {"ctx": sibling})

    ext[core] = jnp.zeros((2, half, HD, HD), jnp.float32)
    scan_begin(1)
    for c in pairs[1:]:
        c.start()
    x_pair.start()

    at_row = lax.broadcasted_iota(jnp.int32, (length, length), 0)
    at_col = lax.broadcasted_iota(jnp.int32, (length, length), 1)
    lower = at_row >= at_col
    upper = at_row <= at_col

    def value_inside(heads_now):
        for h in heads_now:
            score_t = jnp.where(upper, scale * dot(k[:, cols(h)], q[:, cols(h)], NT), 0.0)
            acc[:, cols(h)] = dot(score_t.astype(jnp.bfloat16), g[:, cols(h)], NN)

    value_inside(range(half))
    xt[:, :length] = jnp.transpose(xs[...]).astype(jnp.bfloat16)
    if bits > 0:
        for c in range(half):
            scan_take(1, 0, c)
    scan_begin(0)
    value_inside(range(half, heads))
    x_pair.wait_recv()
    xt[:, length:] = jnp.transpose(xsib[...]).astype(jnp.bfloat16)
    for i in range(1, bits):
        for c in range(half):
            scan_take(1, i, c)
    share(core, 1).start()
    pairs_in[2].wait_recv()
    share(1 - core, 1).wait_recv()

    second = core.astype(jnp.float32)
    first = 1.0 - second

    def suffix(h):
        a, i = h // half, h % half
        return (scale * (ext[a, 1, i] + first * sib[a, 1, i])).astype(jnp.bfloat16)

    def prefix(h):
        a, i = h // half, h % half
        return (scale * (ext[a, 0, i] + second * sib[a, 0, i])).astype(jnp.bfloat16)

    for h in range(heads):
        out = acc[:, cols(h)] + dot(k[:, cols(h)], suffix(h), NN)
        dv[:, cols(h)] = out.astype(jnp.bfloat16)
    for j in range(n):
        dvs[j % 2, j // 2] = dv[:, j * cb:(j + 1) * cb].astype(jnp.float32)
    value = remote(dvs.at[1 - core], dvr, d_send, d_recv, {"ctx": sibling})
    value.start()
    value.wait_recv()

    def chunk(c):
        return lax.rem(row + c + 1, m)

    def halve(s, c, i):
        lo = 1 << (bits - 1 - i)
        d = chunk(c)
        return remote(
            wt.at[s, d, pl.ds(lo, lo)], wr.at[s, d, pl.ds(lo, lo)],
            r_send.at[s, c, i], r_recv.at[s, c, i], {"ctx": flip(1 << orders[s][i]) * 2 + core},
        )

    def across(s, c):
        return remote(
            wt.at[s, chunk(c), 0], wrecv.at[s, c], w_send.at[s, c], w_recv.at[s, c],
            {"dp": chunk(c)},
        )

    def advance(s, c, i):
        d = chunk(c)
        if i > 0:
            lo = 1 << (bits - i)
            halve(s, c, i - 1).wait_recv()
            wt[s, d, 0:lo] += wr[s, d, lo:2 * lo]
        if i < bits:
            halve(s, c, i).start()
        elif c < m - 1:
            across(s, c).start()

    def tiles(masks):
        both = jnp.concatenate([
            jnp.concatenate([dvs[core, flip(mask)], dvr[flip(mask)]], 0).astype(jnp.bfloat16)
            for mask in masks
        ], 1)
        made = dot(xt[...], both, NN)
        for at, mask in enumerate(masks):
            for d in range(m):
                for s in range(2):
                    lo = d * rows + s * part
                    wt[s, d, place(s, mask)] = made[lo:lo + part, at * cb:(at + 1) * cb]

    masks = [*range(chips - 1, 0, -2), *range(chips - 2, -1, -2)]
    wide = 2 if chips > 1 else 1
    ready, begun = set(), set()
    for at in range(0, chips, wide):
        tiles(masks[at:at + wide])
        ready.update(masks[at:at + wide])
        for s in range(2):
            need = {r for r in range(chips) if bits == 0 or r >> orders[s][0] & 1}
            if need <= ready and s not in begun:
                begun.add(s)
                advance(s, 0, 0)
    for s in range(2):
        if bits > 0 and m > 1:
            advance(s, 1, 0)

    def key_out(heads_now):
        for h in heads_now:
            grad = jnp.where(lower, scale * dot(g[:, cols(h)], v[:, cols(h)], NT), 0.0)
            gw[h] = grad.astype(jnp.bfloat16)
            out = dot(gw[h], q[:, cols(h)], TN) + dot(v[:, cols(h)], suffix(h), NT)
            dk[:, cols(h)] = out.astype(jnp.bfloat16)

    def prefix_begin():
        if bits > 0:
            for c in range(half):
                scan_take(0, 0, c)

    def prefix_in():
        for i in range(1, bits):
            for c in range(half):
                scan_take(0, i, c)
        share(core, 0).start()

    def query_out(heads_now):
        for h in heads_now:
            out = dot(gw[h], k[:, cols(h)], NN) + dot(g[:, cols(h)], prefix(h), NT)
            dq[:, cols(h)] = out.astype(jnp.bfloat16)

    def prefix_done():
        pairs_in[3].wait_recv()
        share(1 - core, 0).wait_recv()
        query_out(range(half))

    pieces = [
        lambda: key_out(range(half)),
        lambda: (prefix_begin(), key_out(range(half, heads))),
        prefix_in,
        prefix_done,
        lambda: query_out(range(half, heads)),
    ]
    lead = 1 if bits > 0 else 0
    for t in range(1, m + bits):
        for i in range(bits + 1):
            c = t - i + (lead if i == 0 else 0)
            for s in range(2):
                if 0 <= c < m:
                    advance(s, c, i)
            if i == 0 and pieces:
                pieces.pop(0)()
    for piece in pieces:
        piece()
    for s in range(2):
        out = wt[s, row, 0]
        for c in range(m - 1):
            across(s, c).wait_recv()
            out = out + wrecv[s, c]
        w[s * part:(s + 1) * part] = out * rscale

    for c in pairs + [x_pair, share(core, 0), share(core, 1), value]:
        c.wait_send()
    for kind in range(2):
        for i in range(bits):
            @pl.when(sends(kind, i))
            def _():
                for c in range(half):
                    scan_copy(kind, i, c).wait_send()
    for s in range(2):
        for c in range(m):
            for i in range(bits):
                halve(s, c, i).wait_send()
            if c < m - 1:
                across(s, c).wait_send()


def copy_out(*refs):
    count = (len(refs) - 1) // 3
    sems = refs[-1]

    def copies(source, target, at):
        return [
            pltpu.make_async_copy(refs[source * count + i], refs[target * count + i], sems.at[at, i])
            for i in range(count)
        ]

    into, out = copies(0, 2, 0), copies(2, 1, 1)
    for c in into:
        c.start()
    for i in range(count):
        into[i].wait()
        out[i].start()
    for c in out:
        c.wait()


def on_device(query_heads, key_heads, value_heads, grad_output, layer_input):
    length, width = query_heads.shape[1:]
    wide = layer_input.shape[2]
    n = lax.axis_size("ctx")
    m = lax.axis_size("dp")
    scale = 1.0 / math.sqrt(HD * length * n)
    rscale = 1.0 / math.sqrt(m * length * n)
    heads, chips, cb, rows = width // HD, n // 2, width // n, wide // m
    half, bits = heads // 2, chips.bit_length() - 1
    f32, bf16 = jnp.float32, jnp.bfloat16
    vmem = pl.BlockSpec(memory_space=pltpu.VMEM)
    dma = pltpu.SemaphoreType.DMA
    out = jax.ShapeDtypeStruct((length, width), bf16)
    dq, dk, dv, w = pl.pallas_call(
        functools.partial(kernel, n, m, scale, rscale),
        out_shape=(out, out, out, jax.ShapeDtypeStruct((rows, cb), f32)),
        in_specs=[vmem] * 5,
        out_specs=(vmem,) * 4,
        scratch_shapes=[
            pltpu.VMEM((length, wide), f32),
            pltpu.VMEM((length, wide), f32),
            pltpu.VMEM((wide, 2 * length), bf16),
            pltpu.VMEM((2, 2, half, HD, HD), f32),
            pltpu.VMEM((2, 2, half, HD, HD), f32),
            pltpu.VMEM((2, max(bits, 1), half, HD, HD), f32),
            pltpu.VMEM((2, max(bits, 1), half, HD, HD), f32),
            pltpu.VMEM((2, 2, half, HD, HD), f32),
            pltpu.VMEM((length, width), f32),
            pltpu.VMEM((heads, length, length), bf16),
            pltpu.VMEM((2, chips, length, cb), f32),
            pltpu.VMEM((chips, length, cb), f32),
            pltpu.VMEM((2, m, chips, rows // 2, cb), f32),
            pltpu.VMEM((2, m, chips, rows // 2, cb), f32),
            pltpu.VMEM((2, max(m - 1, 1), rows // 2, cb), f32),
            dma, dma,
            dma((4,)), dma((4,)),
            dma((2, max(bits, 1), half)), dma((2, max(bits, 1), half)),
            dma((2,)), dma((2,)),
            dma, dma,
            dma((2, m, max(bits, 1))), dma((2, m, max(bits, 1))),
            dma((2, max(m - 1, 1))), dma((2, max(m - 1, 1))),
        ],
        compiler_params=pltpu.CompilerParams(
            collective_id=0, has_side_effects=True, vmem_limit_bytes=56 * 2**20
        ),
    )(query_heads[0], key_heads[0], value_heads[0], grad_output[0], layer_input[0])
    made = (dq, dk, dv, w)
    dq, dk, dv, w = pl.pallas_call(
        copy_out,
        out_shape=tuple(jax.ShapeDtypeStruct(r.shape, r.dtype) for r in made),
        in_specs=[pl.BlockSpec(memory_space=pltpu.HBM)] * len(made),
        out_specs=(pl.BlockSpec(memory_space=pltpu.HBM),) * len(made),
        scratch_shapes=[pltpu.VMEM(r.shape, r.dtype) for r in made] + [dma((2, len(made)))],
    )(*made)
    return dq[None], dk[None], dv[None], w


def solution(mesh):
    spec = P("dp", "ctx", None)
    return jax.shard_map(
        on_device, mesh=mesh, in_specs=(spec,) * 5,
        out_specs=(spec, spec, spec, P("dp", "ctx")), check_vma=False,
    )
```

```python
import functools
import math

import jax
import jax.numpy as jnp
from jax import lax
from jax.experimental import pallas as pl
from jax.experimental.pallas import tpu as pltpu
from jax.sharding import PartitionSpec as P

HD = 128
NN = (((1,), (0,)), ((), ()))
NT = (((1,), (1,)), ((), ()))
TN = (((0,), (0,)), ((), ()))


def dot(a, b, dims):
    return lax.dot_general(a, b, dims, preferred_element_type=jnp.float32)


def kernel(
    n, m, scale, rscale,
    q, k, v, g, x,
    dq, dk, dv, w,
    xs, xsib, xt, st, sib, tot, srecv, ext, acc, dvs, dvr, wt, wr, wrecv,
    x_send, x_recv, p_send, p_recv, s_send, s_recv, e_send, e_recv,
    d_send, d_recv, r_send, r_recv, w_send, w_recv,
):
    length, width = q.shape
    heads = width // HD
    half = heads // 2
    chips = n // 2
    cb = dvs.shape[3]
    rows = w.shape[0]
    part = rows // 2
    bits = chips.bit_length() - 1
    me = lax.axis_index("ctx")
    row = lax.axis_index("dp")
    core = lax.rem(me, 2)
    chip = me // 2
    sibling = me + 1 - 2 * core

    def flip(mask):
        out = chip
        for b in range(bits):
            if mask >> b & 1:
                out = out + (1 << b) * (1 - 2 * lax.rem(chip // (1 << b), 2))
        return out

    def remote(src, dst, send, recv, to):
        return pltpu.make_async_remote_copy(
            src_ref=src, dst_ref=dst, send_sem=send, recv_sem=recv,
            device_id=to, device_id_type=pl.DeviceIdType.MESH,
        )

    orders = ([*range(bits)], [*range(bits - 1, -1, -1)])

    def place(s, mask):
        return sum((mask >> b & 1) << (bits - 1 - i) for i, b in enumerate(orders[s]))

    barrier = pltpu.get_barrier_semaphore()
    for j in range(1, n):
        pl.semaphore_signal(
            barrier, inc=1, device_id={"ctx": lax.rem(me + j, n)},
            device_id_type=pl.DeviceIdType.MESH,
        )
    for j in range(1, m):
        pl.semaphore_signal(
            barrier, inc=1, device_id={"dp": lax.rem(row + j, m)},
            device_id_type=pl.DeviceIdType.MESH,
        )

    def cols(h):
        return slice(h * HD, (h + 1) * HD)

    for h in range(heads):
        a, i = h // half, h % half
        st[a, 0, i] = dot(k[:, cols(h)], v[:, cols(h)], TN)
        st[a, 1, i] = dot(q[:, cols(h)], g[:, cols(h)], TN)
    xs[...] = x[...].astype(jnp.float32)
    pl.semaphore_wait(barrier, n - 1 + m - 1)

    pair = [
        remote(st.at[1 - core], sib.at[1 - core], p_send.at[0], p_recv.at[0], {"ctx": sibling}),
        remote(st.at[core], sib.at[core], p_send.at[1], p_recv.at[1], {"ctx": sibling}),
    ]
    pair_in = remote(st.at[core], sib.at[core], p_send.at[0], p_recv.at[0], {"ctx": sibling})
    for c in pair:
        c.start()
    x_pair = remote(xs, xsib, x_send, x_recv, {"ctx": sibling})
    pair_in.wait_recv()
    tot[...] = st[core] + sib[core]
    states = []
    for j in range(1, chips):
        wrap = (chip + j) // chips
        to = (chip + j - chips * wrap) * 2 + core
        c = remote(tot.at[wrap], srecv.at[j - 1], s_send.at[j - 1], s_recv.at[j - 1], {"ctx": to})
        c.start()
        states.append(c)
    x_pair.start()

    at_row = lax.broadcasted_iota(jnp.int32, (length, length), 0)
    at_col = lax.broadcasted_iota(jnp.int32, (length, length), 1)
    lower = at_row >= at_col
    upper = at_row <= at_col
    for h in range(heads):
        qh, kh, gh = (r[:, cols(h)] for r in (q, k, g))
        score_t = jnp.where(upper, scale * dot(kh, qh, NT), 0.0).astype(jnp.bfloat16)
        acc[:, cols(h)] = dot(score_t, gh, NN)

    xt[:, :length] = jnp.transpose(xs[...]).astype(jnp.bfloat16)
    x_pair.wait_recv()
    xt[:, length:] = jnp.transpose(xsib[...]).astype(jnp.bfloat16)

    ext[core] = jnp.zeros_like(tot)
    for j in range(1, chips):
        kind = 1 - (chip - j + chips) // chips
        states[j - 1].wait_recv()
        ext[core, kind] += srecv[j - 1]
    share = remote(ext.at[core], ext.at[core], e_send, e_recv, {"ctx": sibling})
    share_in = remote(ext.at[1 - core], ext.at[1 - core], e_send, e_recv, {"ctx": sibling})
    share.start()
    pair_rest = remote(st.at[1 - core], sib.at[1 - core], p_send.at[1], p_recv.at[1], {"ctx": sibling})
    pair_rest.wait_recv()
    share_in.wait_recv()

    second = core.astype(jnp.float32)
    first = 1.0 - second

    def suffix(h):
        a, i = h // half, h % half
        return (scale * (ext[a, 1, i] + first * sib[a, 1, i])).astype(jnp.bfloat16)

    def prefix(h):
        a, i = h // half, h % half
        return (scale * (ext[a, 0, i] + second * sib[a, 0, i])).astype(jnp.bfloat16)

    for h in range(heads):
        out = acc[:, cols(h)] + dot(k[:, cols(h)], suffix(h), NN)
        dv[:, cols(h)] = out.astype(jnp.bfloat16)
    for j in range(n):
        dvs[j % 2, j // 2] = dv[:, j * cb:(j + 1) * cb].astype(jnp.float32)
    value = remote(dvs.at[1 - core], dvr, d_send, d_recv, {"ctx": sibling})
    value.start()
    value.wait_recv()

    for mask in range(chips - 1, -1, -1):
        to = flip(mask)
        both = jnp.concatenate([dvs[core, to], dvr[to]], 0).astype(jnp.bfloat16)
        tile = dot(xt[...], both, NN)
        for d in range(m):
            for s in range(2):
                lo = d * rows + s * part
                wt[s, d, place(s, mask)] = tile[lo:lo + part]

    def chunk(c):
        return lax.rem(row + c + 1, m)

    def halve(s, c, i):
        lo = 1 << (bits - 1 - i)
        d = chunk(c)
        return remote(
            wt.at[s, d, pl.ds(lo, lo)], wr.at[s, d, pl.ds(lo, lo)],
            r_send.at[s, c, i], r_recv.at[s, c, i], {"ctx": flip(1 << orders[s][i]) * 2 + core},
        )

    def across(s, c):
        return remote(
            wt.at[s, chunk(c), 0], wrecv.at[s, c], w_send.at[s, c], w_recv.at[s, c],
            {"dp": chunk(c)},
        )

    def advance(s, c, i):
        d = chunk(c)
        if i > 0:
            lo = 1 << (bits - i)
            halve(s, c, i - 1).wait_recv()
            wt[s, d, 0:lo] += wr[s, d, lo:2 * lo]
        if i < bits:
            halve(s, c, i).start()
        elif c < m - 1:
            across(s, c).start()

    def step(t):
        for i in range(bits + 1):
            for s in range(2):
                if 0 <= t - i < m:
                    advance(s, t - i, i)

    for s in range(2):
        advance(s, 0, 0)

    def inputs_out(h):
        qh, kh, vh, gh = (r[:, cols(h)] for r in (q, k, v, g))
        grad = jnp.where(lower, scale * dot(gh, vh, NT), 0.0).astype(jnp.bfloat16)
        dq[:, cols(h)] = (dot(grad, kh, NN) + dot(gh, prefix(h), NT)).astype(jnp.bfloat16)
        dk[:, cols(h)] = (dot(grad, qh, TN) + dot(vh, suffix(h), NT)).astype(jnp.bfloat16)

    todo = [*range(heads)]
    for t in range(1, m + bits):
        for i in range(bits + 1):
            for s in range(2):
                if 0 <= t - i < m:
                    advance(s, t - i, i)
            if i == 0:
                for h in todo[:2]:
                    inputs_out(h)
                todo = todo[2:]
    for h in todo:
        inputs_out(h)
    for s in range(2):
        out = wt[s, row, 0]
        for c in range(m - 1):
            across(s, c).wait_recv()
            out = out + wrecv[s, c]
        w[s * part:(s + 1) * part] = out * rscale

    for c in pair + states + [x_pair, share, value]:
        c.wait_send()
    for s in range(2):
        for c in range(m):
            for i in range(bits):
                halve(s, c, i).wait_send()
            if c < m - 1:
                across(s, c).wait_send()


def copy_out(*refs):
    count = (len(refs) - 1) // 3
    sems = refs[-1]

    def copies(source, target, at):
        return [
            pltpu.make_async_copy(refs[source * count + i], refs[target * count + i], sems.at[at, i])
            for i in range(count)
        ]

    into, out = copies(0, 2, 0), copies(2, 1, 1)
    for c in into:
        c.start()
    for i in range(count):
        into[i].wait()
        out[i].start()
    for c in out:
        c.wait()


def on_device(query_heads, key_heads, value_heads, grad_output, layer_input):
    length, width = query_heads.shape[1:]
    wide = layer_input.shape[2]
    n = lax.axis_size("ctx")
    m = lax.axis_size("dp")
    scale = 1.0 / math.sqrt(HD * length * n)
    rscale = 1.0 / math.sqrt(m * length * n)
    heads, chips, cb, rows = width // HD, n // 2, width // n, wide // m
    half, bits = heads // 2, chips.bit_length() - 1
    f32, bf16 = jnp.float32, jnp.bfloat16
    vmem = pl.BlockSpec(memory_space=pltpu.VMEM)
    dma = pltpu.SemaphoreType.DMA
    out = jax.ShapeDtypeStruct((length, width), bf16)
    dq, dk, dv, w = pl.pallas_call(
        functools.partial(kernel, n, m, scale, rscale),
        out_shape=(out, out, out, jax.ShapeDtypeStruct((rows, cb), f32)),
        in_specs=[vmem] * 5,
        out_specs=(vmem,) * 4,
        scratch_shapes=[
            pltpu.VMEM((length, wide), f32),
            pltpu.VMEM((length, wide), f32),
            pltpu.VMEM((wide, 2 * length), bf16),
            pltpu.VMEM((2, 2, half, HD, HD), f32),
            pltpu.VMEM((2, 2, half, HD, HD), f32),
            pltpu.VMEM((2, half, HD, HD), f32),
            pltpu.VMEM((max(chips - 1, 1), half, HD, HD), f32),
            pltpu.VMEM((2, 2, half, HD, HD), f32),
            pltpu.VMEM((length, width), f32),
            pltpu.VMEM((2, chips, length, cb), f32),
            pltpu.VMEM((chips, length, cb), f32),
            pltpu.VMEM((2, m, chips, rows // 2, cb), f32),
            pltpu.VMEM((2, m, chips, rows // 2, cb), f32),
            pltpu.VMEM((2, max(m - 1, 1), rows // 2, cb), f32),
            dma, dma,
            dma((2,)), dma((2,)),
            dma((max(chips - 1, 1),)), dma((max(chips - 1, 1),)),
            dma, dma,
            dma, dma,
            dma((2, m, max(bits, 1))), dma((2, m, max(bits, 1))),
            dma((2, max(m - 1, 1))), dma((2, max(m - 1, 1))),
        ],
        compiler_params=pltpu.CompilerParams(
            collective_id=0, has_side_effects=True, vmem_limit_bytes=56 * 2**20
        ),
    )(query_heads[0], key_heads[0], value_heads[0], grad_output[0], layer_input[0])
    made = (dq, dk, dv, w)
    dq, dk, dv, w = pl.pallas_call(
        copy_out,
        out_shape=tuple(jax.ShapeDtypeStruct(r.shape, r.dtype) for r in made),
        in_specs=[pl.BlockSpec(memory_space=pltpu.HBM)] * len(made),
        out_specs=(pl.BlockSpec(memory_space=pltpu.HBM),) * len(made),
        scratch_shapes=[pltpu.VMEM(r.shape, r.dtype) for r in made] + [dma((2, len(made)))],
    )(*made)
    return dq[None], dk[None], dv[None], w


def solution(mesh):
    spec = P("dp", "ctx", None)
    return jax.shard_map(
        on_device, mesh=mesh, in_specs=(spec,) * 5,
        out_specs=(spec, spec, spec, P("dp", "ctx")), check_vma=False,
    )
```
